512 devices in a mesh: ctx: 64 (over y, z), kv: 8 (over x, core).
Axes of the slice: x: 4, y: 8, z: 8, core: 2. Of those that a mesh axis runs over, the one named last changes fastest.
Arguments:
- queries: bfloat16 [16384, 64, 128], P(('ctx', 'kv')), may hold values from -150 to 150
- keys: bfloat16 [16384, 8, 128], P(('ctx', 'kv')), may hold values from -5 to 5
- values: bfloat16 [16384, 8, 128], P(('ctx', 'kv')), may hold values from -6 to 6
- doc_ids: int32 [16384], P('ctx'), may hold values from 0 to 15, never falling along the last dimension, each value on 1 to 8448 neighbouring positions
Outputs:
- attended: bfloat16 [16384, 64, 128], P(('ctx', 'kv'))
The draws below stay inside these ranges and needn't reach their ends.
Inputs may be any that keep to these rules, and one draw needn't show every extreme that they name: `doc_ids`: document numbers never fall along the sequence; each document holds 1 to 8448 tokens, and one holds exactly 8448.
All inputs are finite; a program needn't handle non-finite values.
Results may differ from the reference program's by a relative error of at most 0.0055.
Values may be sent and summed in bfloat16 or wider, within the bound.
A program may use at most 64 MiB of HBM per device.

```python
import math
import jax
import jax.numpy as jnp
import numpy as np
from jax import lax

HEADS = 64
KV_HEADS = 8
HEAD_DIM = 128
TOKENS = 16384
MOST = 8448
DOCS = 16


def shared_keys(key):
    return jax.random.truncated_normal(key, -5.0, 5.0, (TOKENS, KV_HEADS, HEAD_DIM), jnp.float32)


def draw_keys(key, part):
    return shared_keys(key).astype(jnp.bfloat16)


def draw_queries(key, part):
    key = jax.random.fold_in(key, 7)
    first_key = jax.random.fold_in(key, 0)
    drawn = jax.random.truncated_normal(first_key, -5.0, 5.0, (TOKENS, HEADS, HEAD_DIM), jnp.float32)
    return drawn.astype(jnp.bfloat16)


def steps_of(stream_key, extent, pieces, smallest, high):
    loudness, own = 1.0, jax.random.fold_in(stream_key, 6)
    for axis_at, shards_of in pieces:
        draws = jnp.exp(jax.random.uniform(jax.random.fold_in(own, axis_at), (shards_of,), jnp.float32, smallest / len(pieces), high / len(pieces)))
        loudness = loudness * jnp.repeat(draws, extent[axis_at] // shards_of).reshape([-1 if axis == axis_at else 1 for axis in range(len(extent))])
    return loudness


def profile(number_of, total, limit, slope):
    weights = [(1 << 20) // math.isqrt(grade ** slope) + 1 for grade in range(2, number_of + 1)]
    surplus, counts = total - limit - (number_of - 1), [1] * (number_of - 1)
    while surplus > 0:
        candidates = [i for i in range(number_of - 1) if counts[i] < limit]
        pool, left = sum([weights[i] for i in candidates]), surplus
        for i in candidates:
            extra = min(limit - counts[i], max(1, left * weights[i] // pool), surplus)
            counts[i] = counts[i] + extra
            surplus = surplus - extra
    return np.array([limit] + counts)


def ragged(own_key, count, total, reach, skew):
    if count == 2:
        one = jax.random.randint(own_key, (), max(1, total - reach), min(reach, total - 1) + 1)
        return jnp.stack([one, total - one])
    lengths = jnp.asarray(profile(count, total, reach, skew), jnp.int32)
    couples = (count - 1) // 2
    giver, sink = lengths[1:1 + 2 * couples:2], lengths[2:2 + 2 * couples:2]
    margin = jnp.minimum(giver - 1, reach - sink)
    moved = jax.random.randint(jax.random.fold_in(own_key, 1), (couples,), 0, 1 << 20) % (margin + 1)
    lengths = lengths.at[1:1 + 2 * couples:2].set(giver - moved).at[2:2 + 2 * couples:2].set(sink + moved)
    return lengths[jax.random.permutation(jax.random.fold_in(own_key, 2), count)]


def scatter_about(key, dims, scale, most, cuts=(), held_as=jnp.bfloat16):
    array = jax.random.normal(key, dims, jnp.float32) * scale
    if len(cuts) > 0:
        array = steps_of(key, dims, cuts, -0.22, 0.18) * array
    return jnp.clip(array, min=-most, max=most).astype(held_as)


def setup_inputs(seed: int = 0) -> dict:
    arg_keys = jax.random.split(jax.random.key(seed), 5)
    return {
        "queries": draw_queries(jax.random.fold_in(arg_keys[4], 71), 0),
        "keys": draw_keys(jax.random.fold_in(arg_keys[4], 71), 0),
        "values": scatter_about(arg_keys[2], (TOKENS, KV_HEADS, HEAD_DIM), 1.0, 6.0, ((0, 512),)),
        "doc_ids": jnp.searchsorted(jnp.cumsum(ragged(arg_keys[3], DOCS, TOKENS, MOST, 2)), jnp.arange(TOKENS), side="right").astype(jnp.int32),
    }


def reference(queries, keys, values, doc_ids):
    group = HEADS // KV_HEADS
    block = math.gcd(TOKENS, 256)
    scale = 1.0 / math.sqrt(HEAD_DIM)
    pad_keys = jnp.concatenate([jnp.zeros((MOST, KV_HEADS, HEAD_DIM), jnp.bfloat16), keys], axis=0)
    pad_values = jnp.concatenate([jnp.zeros((MOST, KV_HEADS, HEAD_DIM), jnp.bfloat16), values], axis=0)
    pad_ids = jnp.concatenate([jnp.full((MOST,), -1, jnp.int32), doc_ids.astype(jnp.int32)], axis=0)

    def one_block(index):
        first = (index * block).astype(jnp.int32)
        query_rows = lax.dynamic_slice_in_dim(queries, first, block, 0)
        key_rows = lax.dynamic_slice_in_dim(pad_keys, first, MOST + block, 0)
        value_rows = lax.dynamic_slice_in_dim(pad_values, first, MOST + block, 0)
        key_ids = lax.dynamic_slice_in_dim(pad_ids, first, MOST + block, 0)
        query_ids = lax.dynamic_slice_in_dim(doc_ids.astype(jnp.int32), first, block, 0)
        query_pos = first + jnp.arange(block, dtype=jnp.int32)
        key_pos = first - MOST + jnp.arange(MOST + block, dtype=jnp.int32)
        grouped = query_rows.reshape(block, KV_HEADS, group, HEAD_DIM).astype(jnp.float32)
        scores = jnp.einsum('bgqd,kgd->gqbk', grouped, key_rows.astype(jnp.float32)) * scale
        mask = (key_ids[None, :] == query_ids[:, None]) & (key_pos[None, :] <= query_pos[:, None])
        scores = jnp.where(mask, scores, -1e+30)
        peak = lax.optimization_barrier(jnp.max(scores, axis=-1, keepdims=True))
        expd = jnp.where(mask, jnp.exp(scores - peak), 0.0)
        total = lax.optimization_barrier(jnp.sum(expd, axis=-1))
        weights = expd.astype(jnp.bfloat16)
        summed = jnp.einsum('gqbk,kgd->bgqd', weights.astype(jnp.float32), value_rows.astype(jnp.float32))
        result = summed / jnp.transpose(total, (2, 0, 1))[..., None]
        return result.reshape(block, HEADS, HEAD_DIM).astype(jnp.bfloat16)
    blocks = lax.map(one_block, jnp.arange(TOKENS // block, dtype=jnp.int32))
    return blocks.reshape(TOKENS, HEADS, HEAD_DIM)
```

```python
import math

import jax
import jax.numpy as jnp
from jax import lax
from jax.experimental import pallas as pl
from jax.experimental.pallas import tpu as pltpu
from jax.sharding import PartitionSpec as P

ROWS, COLS, XS, CS = 8, 8, 4, 2
TOK, HD, PG = 32, 128, 8
QROWS = TOK * PG
BLK = XS * CS * TOK
ROWTOK = COLS * BLK
BIG = 1e30
C = math.log2(math.e) / math.sqrt(HD)
MESH = pl.DeviceIdType.MESH
F32, BF16 = jnp.float32, jnp.bfloat16
NT = (((1,), (1,)), ((), ()))
NN = (((1,), (0,)), ((), ()))


def wide(x, k):
    return jnp.concatenate([x] * k, axis=1)


def kernel(
    qs, kvs, cnt, o_ref,
    qbuf, kvbuf, qa, kaug, acc, top, sbuf, obuf, cy, cz,
    loc, kva_s, kva_r, q_s, q_r, cy_s, cy_r, cz_s, cz_r, o_s, o_r,
    x0_s, x0_r, vz_s, vz_r, kz_s, kz_r, vx_s, vx_r, sib_s, sib_r,
):
    ctx, kv = lax.axis_index("ctx"), lax.axis_index("kv")
    y, z, x, c = ctx // COLS, ctx % COLS, kv // CS, kv % CS

    def on_y(d):
        return (((y + d) % ROWS) * COLS + z, kv)

    def on_z(d):
        return (y * COLS + (z + d) % COLS, kv)

    def on_x(d):
        return (ctx, ((x + d) % XS) * CS + c)

    sibling = (ctx, x * CS + 1 - c)

    def remote(src, dst, ss, rs, dev):
        return pltpu.make_async_remote_copy(
            src_ref=src, dst_ref=dst, send_sem=ss, recv_sem=rs, device_id=dev, device_id_type=MESH
        )

    def kva(d):
        return remote(kvs.at[(y + d) % ROWS], kvbuf.at[:, y, z, x, c], kva_s.at[d], kva_r.at[d], on_y(d))

    def qcopy(d):
        return remote(qs.at[(y + d) % ROWS], qbuf.at[y], q_s.at[d], q_r.at[d], on_y(d))

    def cycopy(d):
        return remote(cnt, cy.at[y], cy_s.at[d], cy_r.at[d], on_y(d))

    def czcopy(d):
        return remote(cz.at[z], cz.at[z], cz_s.at[d], cz_r.at[d], on_z(d))

    def x0(d):
        at = kvbuf.at[:, :, z, x, c]
        return remote(at, at, x0_s.at[d], x0_r.at[d], on_x(d))

    def rows_of(half):
        return pl.ds(0, ROWS) if half is None else pl.ds(half * (ROWS // 2), ROWS // 2)

    def vz(way, hop, half=None):
        zz = (z + (COLS + 1 - hop if way == 0 else hop - 1)) % COLS
        at = kvbuf.at[1, rows_of(half), zz, x, c]
        return remote(at, at, vz_s.at[way, hop], vz_r.at[way, hop], on_z(1 if way == 0 else COLS - 1))

    def kz(way, hop, half=None):
        zz = (z + (COLS + 1 - hop if way == 0 else hop - 1)) % COLS
        at = kvbuf.at[0, rows_of(half), zz, :, c]
        return remote(at, at, kz_s.at[way, hop], kz_r.at[way, hop], on_z(1 if way == 0 else COLS - 1))

    def vx(off, d):
        at = kvbuf.at[1, :, (z + off) % COLS, x, c]
        return remote(at, at, vx_s.at[off, d], vx_r.at[off, d], on_x(d))

    def sib(off):
        at = kvbuf.at[:, :, (z + off) % COLS, :, c]
        return remote(at, at, sib_s.at[off], sib_r.at[off], sibling)

    def ocopy(d):
        return remote(obuf.at[(y + d) % ROWS], o_ref.at[y], o_s.at[d], o_r.at[d], on_y(d))

    barrier = pltpu.get_barrier_semaphore()
    peers = [on_y(d) for d in range(1, ROWS)] + [on_z(d) for d in range(1, COLS)]
    peers += [on_x(d) for d in range(1, XS)] + [sibling]
    for dev in peers:
        pl.semaphore_signal(barrier, inc=1, device_id=dev, device_id_type=MESH)
    pl.semaphore_wait(barrier, len(peers))

    order = (1, 7, 2, 6, 3, 5, 4)
    for d in order:
        kva(d).start()
    for d in order:
        cycopy(d).start()
    own_kv = pltpu.make_async_copy(kvs.at[y], kvbuf.at[:, y, z, x, c], loc.at[0])
    own_q = pltpu.make_async_copy(qs.at[y], qbuf.at[y], loc.at[1])
    own_kv.start()
    own_q.start()
    for d in order:
        qcopy(d).start()
    for d in order:
        kva(d).wait_recv()
    own_kv.wait()

    vz(0, 1).start()
    vz(1, 1).start()
    for d in (1, 3, 2):
        x0(d).start()
    for d in order:
        cycopy(d).wait_recv()
    cy[y] = cnt[...]
    line = cy[0]
    for r in range(1, ROWS):
        line = line + cy[r]
    cz[z] = line
    for d in order:
        czcopy(d).start()

    def v_step(hop):
        vz(0, hop).wait_recv()
        vz(1, hop).wait_recv()
        if hop < 3:
            vz(0, hop + 1).start()
            vz(1, hop + 1).start()
        else:
            vz(0, 4, 0).start()
            vz(1, 4, 1).start()
        for off in (COLS - hop, hop):
            for d in (1, 3, 2):
                vx(off, d).start()

    v_step(1)
    for d in (1, 3, 2):
        x0(d).wait_recv()
    kz(0, 1).start()
    kz(1, 1).start()
    sib(0).start()
    v_step(2)

    for d in order:
        czcopy(d).wait_recv()
    total = cz[0]
    for r in range(1, COLS):
        total = total + cz[r]
    first, last = total[0:1], total[4:5]
    lane = lax.broadcasted_iota(jnp.int32, (1, HD), 1)
    sign = jnp.where(lane < 16, 1, -1)
    row256 = lax.broadcasted_iota(jnp.int32, (BLK, HD), 0)
    here = BLK * z + (CS * TOK) * x + TOK * c

    @pl.loop(0, ROWS)
    def _(r):
        pos = ROWTOK * r + here + row256 // PG
        same = (pos >= first) & (pos < last) & (lane < 16)
        qa[r] = jnp.where(same | (lane == 16 + r), -BIG, 0.0).astype(BF16)

    @pl.loop(0, COLS)
    def _(zk):
        bound = ROWTOK * (lane - 16 + jnp.where(zk < z, 1, 0))
        limit = jnp.where(lane < 16, first, 1 - bound)

        @pl.loop(0, ROWS)
        def _(r):
            pos = ROWTOK * r + BLK * zk + row256
            kaug[zk, r] = jnp.where(pos * sign < limit, 1.0, 0.0).astype(BF16)

    v_step(3)
    vz(0, 4, 0).wait_recv()
    vz(1, 4, 1).wait_recv()
    for d in (1, 3, 2):
        vx(4, d).start()
    for d in order:
        qcopy(d).wait_recv()
    own_q.wait()
    sib(0).wait_recv()

    def s_tile(r, r0, zk):
        q = jnp.concatenate([qbuf[r], qa[r]], axis=1)
        k = kvbuf[0, pl.ds(r0, 2), zk].reshape(2 * BLK, HD)
        k = jnp.concatenate([k, kaug[zk, pl.ds(r0, 2)].reshape(2 * BLK, HD)], axis=1)
        return lax.dot_general(q, k, NT, preferred_element_type=F32)

    def top_of(s):
        mx = s[:, :HD]
        for j in range(1, s.shape[1] // HD):
            mx = jnp.maximum(mx, s[:, j * HD:(j + 1) * HD])
        return jnp.max(mx, axis=1, keepdims=True)

    def weigh(s, mn, v):
        p = jnp.exp2((s - wide(mn, s.shape[1] // HD)) * C).astype(BF16)
        v = jnp.concatenate([v, jnp.ones_like(v)], axis=1)
        return lax.dot_general(p, v, NN, preferred_element_type=F32)

    def update(r, r0, zk, s):
        old = top[r]
        new = jnp.maximum(old, top_of(s))
        fade = jnp.exp2((old - new) * C)
        top[r] = new
        v = kvbuf[1, pl.ds(r0, 2), zk].reshape(2 * BLK, HD)
        acc[r] = acc[r] * wide(fade, 2) + weigh(s, new, v)

    @pl.loop(0, ROWS)
    def _(r):
        q = jnp.concatenate([qbuf[r], jnp.where(lane < 16, qa[r], 0.0).astype(BF16)], axis=1)
        k = jnp.concatenate([kvbuf[0, r, z].reshape(BLK, HD), kaug[z, r]], axis=1)
        s = lax.dot_general(q, k, NT, preferred_element_type=F32)
        at = (CS * TOK) * x + TOK * c + lax.broadcasted_iota(jnp.int32, (QROWS, BLK), 0) // PG
        s = jnp.where(lax.broadcasted_iota(jnp.int32, (QROWS, BLK), 1) <= at, s, -BIG)
        new = jnp.broadcast_to(top_of(s), (QROWS, HD))
        top[r] = new
        acc[r] = weigh(s, new, kvbuf[1, r, z].reshape(BLK, HD))

    def run(place, tiles, unroll):
        sbuf[0] = s_tile(*place(0))

        @pl.loop(0, tiles // unroll)
        def _(i):
            for u in range(unroll):
                f = i * unroll + u
                sbuf[(u + 1) % 2] = s_tile(*place(jnp.minimum(f + 1, tiles - 1)))
                update(*place(f), sbuf[u % 2])

    def base(r, zk, spread):
        high = r - jnp.where(zk < z, 0, 1)
        return jnp.maximum(high - spread, 0)

    def most(zk):
        def place(f):
            r = jnp.where(f < 2, f, 2 + (f - 2) // 2)
            r0 = base(r, zk, 3) + jnp.where(f < 2, 0, 2 * (f % 2))
            return r, r0, zk
        return place

    @pl.loop(1, 4)
    def _(k):
        for way in range(2):
            kz(way, k).wait_recv()

        @pl.when(k < 3)
        def _():
            for way in range(2):
                kz(way, k + 1).start()

        @pl.when(k == 3)
        def _():
            for way in range(2):
                kz(way, 4, way).start()

        for off in (COLS - k, k):
            for d in (1, 3, 2):
                vx(off, d).wait_recv()
            sib(off).start()

        @pl.loop(0, 2)
        def _(j):
            @pl.when(j == 1)
            def _():
                sib(COLS - k).wait_recv()

            zk = (z + jnp.where(j == 0, k - 1, COLS - k)) % COLS
            run(most(zk), 14, 14)

        sib(k).wait_recv()

    kz(0, 4, 0).wait_recv()
    kz(1, 4, 1).wait_recv()
    for d in (1, 3, 2):
        vx(4, d).wait_recv()
    sib(4).start()

    before = (z + COLS - 1) % COLS

    @pl.loop(4, ROWS)
    def _(r):
        row = r - 4 - jnp.where(before < z, 0, 1)

        @pl.when(row >= 0)
        def _():
            q = jnp.concatenate([qbuf[r], qa[r]], axis=1)
            k = jnp.concatenate([kvbuf[0, row, before].reshape(BLK, HD), kaug[before, row]], axis=1)
            s = lax.dot_general(q, k, NT, preferred_element_type=F32)
            old = top[r]
            new = jnp.maximum(old, top_of(s))
            top[r] = new
            v = kvbuf[1, row, before].reshape(BLK, HD)
            acc[r] = acc[r] * wide(jnp.exp2((old - new) * C), 2) + weigh(s, new, v)

    sib(4).wait_recv()

    def dist(i):
        return 4 + ((i + 1) // 2) * (1 - 2 * (i % 2))

    def last_place(f):
        r = (y + dist(f // 4)) % ROWS
        zk = (z + 3 + (f % 4) // 2) % COLS
        return r, base(r, zk, 3) + 2 * (f % 2), zk

    sbuf[0] = s_tile(*last_place(0))

    @pl.loop(0, ROWS)
    def _(i):
        d = dist(i)
        r = (y + d) % ROWS
        for u in range(4):
            f = 4 * i + u
            sbuf[(u + 1) % 2] = s_tile(*last_place(jnp.minimum(f + 1, 4 * ROWS - 1)))
            update(*last_place(f), sbuf[u % 2])
        done = acc[r]
        obuf[r] = (done[:, :HD] / done[:, HD:]).astype(BF16)

        @pl.when(d > 0)
        def _():
            ocopy(d).start()

    own_o = pltpu.make_async_copy(obuf.at[y], o_ref.at[y], loc.at[2])
    own_o.start()

    for d in order:
        kva(d).wait_send()
        qcopy(d).wait_send()
        cycopy(d).wait_send()
        czcopy(d).wait_send()
    for way in range(2):
        for hop in (1, 2, 3):
            vz(way, hop).wait_send()
            kz(way, hop).wait_send()
        vz(way, 4, way).wait_send()
        kz(way, 4, way).wait_send()
    for d in range(1, XS):
        x0(d).wait_send()
        for off in range(1, COLS):
            vx(off, d).wait_send()
    for off in range(COLS):
        sib(off).wait_send()
    own_o.wait()
    for d in order:
        ocopy(d).wait()


def attend(queries, keys, values, doc_ids):
    qs = queries.reshape(TOK, ROWS, PG, HD).transpose(1, 0, 2, 3).reshape(ROWS, QROWS, HD)
    kvs = jnp.stack([keys, values]).transpose(2, 0, 1, 3)
    docs = jnp.arange(HD, dtype=jnp.int32)
    below = jnp.sum((doc_ids[:, None] < docs[None, :]).astype(jnp.int32), axis=0)
    upto = jnp.sum((doc_ids[:, None] <= docs[None, :]).astype(jnp.int32), axis=0)
    cnt = jnp.repeat(jnp.stack([below, upto]), 4, axis=0)
    dma = pltpu.SemaphoreType.DMA
    vmem = pl.BlockSpec(memory_space=pltpu.VMEM)
    out = pl.pallas_call(
        kernel,
        out_shape=jax.ShapeDtypeStruct((ROWS, QROWS, HD), BF16),
        in_specs=[vmem, vmem, vmem],
        out_specs=pl.BlockSpec(memory_space=pl.ANY),
        scratch_shapes=[
            pltpu.VMEM((ROWS, QROWS, HD), BF16),
            pltpu.VMEM((2, ROWS, COLS, XS, CS, TOK, HD), BF16),
            pltpu.VMEM((ROWS, QROWS, HD), BF16),
            pltpu.VMEM((COLS, ROWS, BLK, HD), BF16),
            pltpu.VMEM((ROWS, QROWS, 2 * HD), F32),
            pltpu.VMEM((ROWS, QROWS, HD), F32),
            pltpu.VMEM((2, QROWS, 2 * BLK), F32),
            pltpu.VMEM((ROWS, QROWS, HD), BF16),
            pltpu.VMEM((ROWS, 8, HD), jnp.int32),
            pltpu.VMEM((COLS, 8, HD), jnp.int32),
            dma((3,)),
            *[dma((8,))] * 10,
            *[dma((4,))] * 2,
            *[dma((2, 5))] * 4,
            *[dma((8, 4))] * 2,
            *[dma((8,))] * 2,
        ],
        compiler_params=pltpu.CompilerParams(
            collective_id=0, has_side_effects=True, vmem_limit_bytes=50 * 2**20
        ),
        name="attend",
    )(qs, kvs, cnt)
    return out.reshape(ROWS, TOK, PG, HD).transpose(1, 0, 2, 3).reshape(TOK, ROWS * PG, HD)


def solution(mesh):
    tokens = P(("ctx", "kv"), None, None)
    return jax.shard_map(
        attend,
        mesh=mesh,
        in_specs=(tokens, tokens, tokens, P("ctx")),
        out_specs=tokens,
        check_vma=False,
    )
```

```python
import math

import jax
import jax.numpy as jnp
from jax import lax
from jax.experimental import pallas as pl
from jax.experimental.pallas import tpu as pltpu
from jax.sharding import PartitionSpec as P

ROWS, COLS, XS, CS = 8, 8, 4, 2
TOK, HD, PG = 32, 128, 8
QROWS = TOK * PG
BLK = XS * CS * TOK
ROWTOK = COLS * BLK
DOCS = 16
BIG = 1e30
C = math.log2(math.e) / math.sqrt(HD)
MESH = pl.DeviceIdType.MESH
F32, BF16 = jnp.float32, jnp.bfloat16
NT = (((1,), (1,)), ((), ()))
NN = (((1,), (0,)), ((), ()))


LATE = (3, 4, 5)


def wide(x, k):
    return jnp.concatenate([x] * k, axis=1)


def kernel(
    qs, kvs, ids, o_ref,
    qbuf, kvbuf, qa, kaug, acc, top, sbuf, obuf, cy, cz,
    loc, kva_s, kva_r, q_s, q_r, cy_s, cy_r, cz_s, cz_r, o_s, o_r,
    x0_s, x0_r, vz_s, vz_r, kz_s, kz_r, vx_s, vx_r, sib_s, sib_r,
):
    ctx, kv = lax.axis_index("ctx"), lax.axis_index("kv")
    y, z, x, c = ctx // COLS, ctx % COLS, kv // CS, kv % CS

    def on_y(d):
        return (((y + d) % ROWS) * COLS + z, kv)

    def on_z(d):
        return (y * COLS + (z + d) % COLS, kv)

    def on_x(d):
        return (ctx, ((x + d) % XS) * CS + c)

    sibling = (ctx, x * CS + 1 - c)

    def remote(src, dst, ss, rs, dev):
        return pltpu.make_async_remote_copy(
            src_ref=src, dst_ref=dst, send_sem=ss, recv_sem=rs, device_id=dev, device_id_type=MESH
        )

    def kva(d):
        return remote(kvs.at[(y + d) % ROWS], kvbuf.at[:, y, z, x, c], kva_s.at[d], kva_r.at[d], on_y(d))

    def qcopy(d):
        return remote(qs.at[(y + d) % ROWS], qbuf.at[y], q_s.at[d], q_r.at[d], on_y(d))

    def cycopy(d):
        return remote(cy.at[y], cy.at[y], cy_s.at[d], cy_r.at[d], on_y(d))

    def czcopy(d):
        return remote(cz.at[z], cz.at[z], cz_s.at[d], cz_r.at[d], on_z(d))

    def x0(which, d):
        at = kvbuf.at[which, :, z, x, c]
        return remote(at, at, x0_s.at[which, d], x0_r.at[which, d], on_x(d))

    def rows_of(half):
        return pl.ds(0, ROWS) if half is None else pl.ds(half * (ROWS // 2), ROWS // 2)

    def column(way, hop):
        return (z + (COLS + 1 - hop if way == 0 else hop - 1)) % COLS

    def vz(way, hop, half=None):
        at = kvbuf.at[1, rows_of(half), column(way, hop), x, c]
        return remote(at, at, vz_s.at[way, hop], vz_r.at[way, hop], on_z(1 if way == 0 else COLS - 1))

    def kz(way, hop, piece):
        at = kvbuf.at[0, :, column(way, hop), (x + (0, 3, 1, 2)[piece]) % XS, c]
        return remote(
            at, at, kz_s.at[way, hop, piece], kz_r.at[way, hop, piece], on_z(1 if way == 0 else COLS - 1)
        )

    def vx(off, d):
        at = kvbuf.at[1, :, (z + off) % COLS, x, c]
        return remote(at, at, vx_s.at[off, d], vx_r.at[off, d], on_x(d))

    def sib(off):
        at = kvbuf.at[:, :, (z + off) % COLS, :, c]
        return remote(at, at, sib_s.at[off], sib_r.at[off], sibling)

    def ocopy(d):
        return remote(obuf.at[(y + d) % ROWS], o_ref.at[y], o_s.at[d], o_r.at[d], on_y(d))

    barrier = pltpu.get_barrier_semaphore()
    peers = [on_y(d) for d in range(1, ROWS)] + [on_z(d) for d in range(1, COLS)]
    peers += [on_x(d) for d in range(1, XS)] + [sibling]
    for dev in peers:
        pl.semaphore_signal(barrier, inc=1, device_id=dev, device_id_type=MESH)

    lane = lax.broadcasted_iota(jnp.int32, (1, HD), 1)
    below = jnp.where(lane == 0, 0, BLK)
    upto = jnp.full((1, HD), BLK, jnp.int32)
    for d in range(1, DOCS):
        count = jnp.sum(jnp.where(ids[...] < d, 1.0, 0.0), axis=1, keepdims=True)
        count = jnp.sum(count, axis=0, keepdims=True).astype(jnp.int32)
        below = jnp.where(lane == d, count, below)
        upto = jnp.where(lane == d - 1, count, upto)
    row8 = lax.broadcasted_iota(jnp.int32, (8, HD), 0)
    cy[y] = jnp.where(row8 < 4, below, upto)

    pl.semaphore_wait(barrier, len(peers))

    order = (1, 7, 2, 6, 3, 5, 4)
    near = (1, 3, 2)
    ways = (0, 1)
    for d in order:
        kva(d).start()
    for d in order:
        cycopy(d).start()
    own_kv = pltpu.make_async_copy(kvs.at[y], kvbuf.at[:, y, z, x, c], loc.at[0])
    own_q = pltpu.make_async_copy(qs.at[y], qbuf.at[y], loc.at[1])
    own_kv.start()
    own_q.start()
    for d in order:
        qcopy(d).start()
    for d in order:
        kva(d).wait_recv()
    own_kv.wait()

    for way in ways:
        vz(way, 1).start()
    for d in near:
        x0(0, d).start()
    for way in ways:
        kz(way, 1, 0).start()
    for d in near:
        x0(1, d).start()
    for d in order:
        cycopy(d).wait_recv()
    line = cy[0]
    for r in range(1, ROWS):
        line = line + cy[r]
    cz[z] = line
    for d in order:
        czcopy(d).start()
    for piece in (1, 2, 3):
        x0(0, near[piece - 1]).wait_recv()
        for way in ways:
            kz(way, 1, piece).start()

    def v_event(hop):
        for way in ways:
            if hop < 4:
                vz(way, hop).wait_recv()
            else:
                vz(way, 4, way).wait_recv()
            if hop < 3:
                vz(way, hop + 1).start()
            elif hop == 3:
                vz(way, 4, way).start()
        for off in (COLS - hop, hop) if hop < 4 else (4,):
            for d in near:
                vx(off, d).start()

    def k_event(hop, pieces):
        mine = 0 if pieces[0] == 0 else 1
        for piece in pieces:
            for way in ways:
                if hop < 4 or way == mine:
                    kz(way, hop, piece).wait_recv()
                if hop < 3 or (hop == 3 and way == mine):
                    kz(way, hop + 1, piece).start()

    def pass_on(off):
        for d in near:
            vx(off, d).wait_recv()
        sib(off).start()

    v_event(1)
    for d in order:
        czcopy(d).wait_recv()
    total = cz[0]
    for r in range(1, COLS):
        total = total + cz[r]
    first, last = total[0:1], total[4:5]
    sign = jnp.where(lane < DOCS, 1, -1)
    row256 = lax.broadcasted_iota(jnp.int32, (BLK, HD), 0)
    here = BLK * z + (CS * TOK) * x + TOK * c

    @pl.loop(0, ROWS)
    def _(r):
        pos = ROWTOK * r + here + row256 // PG
        same = (pos >= first) & (pos < last) & (lane < DOCS)
        qa[r] = jnp.where(same | (lane == DOCS + r), -BIG, 0.0).astype(BF16)

    @pl.loop(0, COLS)
    def _(zk):
        bound = ROWTOK * (lane - DOCS + jnp.where(zk < z, 1, 0))
        limit = jnp.where(lane < DOCS, first, 1 - bound)

        @pl.loop(0, ROWS)
        def _(r):
            pos = ROWTOK * r + BLK * zk + row256
            kaug[zk, r] = jnp.where(pos * sign < limit, 1.0, 0.0).astype(BF16)

    k_event(1, (0, 1))
    for d in near:
        x0(1, d).wait_recv()
    sib(0).start()

    v_event(2)
    sib(0).wait_recv()

    def s_tile(r, r0, zk):
        q = jnp.concatenate([qbuf[r], qa[r]], axis=1)
        k = kvbuf[0, pl.ds(r0, 2), zk].reshape(2 * BLK, HD)
        k = jnp.concatenate([k, kaug[zk, pl.ds(r0, 2)].reshape(2 * BLK, HD)], axis=1)
        return lax.dot_general(q, k, NT, preferred_element_type=F32)

    def v_tile(r0, zk):
        return kvbuf[1, pl.ds(r0, 2), zk].reshape(2 * BLK, HD)

    def top_of(s):
        mx = s[:, :HD]
        for j in range(1, s.shape[1] // HD):
            mx = jnp.maximum(mx, s[:, j * HD:(j + 1) * HD])
        return jnp.max(mx, axis=1, keepdims=True)

    def weigh(s, mn, v):
        p = jnp.exp2((s - wide(mn, s.shape[1] // HD)) * C).astype(BF16)
        v = jnp.concatenate([v, jnp.ones_like(v)], axis=1)
        return lax.dot_general(p, v, NN, preferred_element_type=F32)

    def update(r, r0, zk, s):
        old = top[r]
        new = jnp.maximum(old, top_of(s))
        fade = jnp.exp2((old - new) * C)
        top[r] = new
        acc[r] = acc[r] * wide(fade, 2) + weigh(s, new, v_tile(r0, zk))

    def base(r, zk, spread):
        high = r - jnp.where(zk < z, 0, 1)
        return jnp.maximum(high - spread, 0)

    @pl.loop(0, ROWS)
    def _(i):
        half = (i + 1) // 2
        d = (half + (i + 1) % 2 * (COLS - 2 * half)) % ROWS

        @pl.when(i == 0)
        def _():
            own_q.wait()

        @pl.when(i > 0)
        def _():
            qcopy(d).wait_recv()

        r = (y + ROWS - d) % ROWS
        r0 = base(r, z, 3)
        q = jnp.concatenate([qbuf[r], jnp.where(lane < DOCS, qa[r], 0.0).astype(BF16)], axis=1)
        k = jnp.concatenate([kvbuf[0, r, z].reshape(BLK, HD), kaug[z, r]], axis=1)
        s = lax.dot_general(q, k, NT, preferred_element_type=F32)
        at = (CS * TOK) * x + TOK * c + lax.broadcasted_iota(jnp.int32, (QROWS, BLK), 0) // PG
        s = jnp.where(lax.broadcasted_iota(jnp.int32, (QROWS, BLK), 1) <= at, s, -BIG)
        s1, s2 = s_tile(r, r0, z), s_tile(r, r0 + 2, z)
        new = jnp.maximum(jnp.maximum(top_of(s), top_of(s1)), top_of(s2))
        new = jnp.broadcast_to(new, (QROWS, HD))
        top[r] = new
        acc[r] = (
            weigh(s, new, kvbuf[1, r, z].reshape(BLK, HD))
            + weigh(s1, new, v_tile(r0, z))
            + weigh(s2, new, v_tile(r0 + 2, z))
        )

        @pl.when(i == 1)
        def _():
            k_event(1, (2, 3))

        @pl.when(i == 3)
        def _():
            v_event(3)

        @pl.when(i == 5)
        def _():
            pass_on(7)

    pass_on(1)
    k_event(2, (0, 1))

    def run(place, tiles):
        sbuf[0] = s_tile(*place(0))
        for f in range(tiles):
            if f + 1 < tiles:
                sbuf[(f + 1) % 2] = s_tile(*place(f + 1))
            update(*place(f), sbuf[f % 2])

    @pl.loop(0, 4)
    def _(g):
        off = jnp.where(g % 2 == 0, COLS - 1 - g // 2, 1 + g // 2)
        zk = (z + off) % COLS
        sib(off).wait_recv()

        def place(f):
            r = f if f < 2 else 2 + (f - 2) // 2
            return r, base(r, zk, 3) + (0 if f < 2 else 2 * (f % 2)), zk

        run(place, 14)

        @pl.when(g == 0)
        def _():
            k_event(2, (2, 3))
            v_event(4)
            pass_on(6)

        @pl.when(g == 1)
        def _():
            k_event(3, (0, 1))
            pass_on(2)

        @pl.when(g == 2)
        def _():
            k_event(3, (2, 3))
            pass_on(5)

        @pl.when(g == 3)
        def _():
            k_event(4, (0, 1))
            k_event(4, (2, 3))
            pass_on(3)
            pass_on(4)

    before = (z + COLS - 1) % COLS

    @pl.loop(4, ROWS)
    def _(r):
        row = r - 4 - jnp.where(before < z, 0, 1)

        @pl.when(row >= 0)
        def _():
            q = jnp.concatenate([qbuf[r], qa[r]], axis=1)
            k = jnp.concatenate([kvbuf[0, row, before].reshape(BLK, HD), kaug[before, row]], axis=1)
            s = lax.dot_general(q, k, NT, preferred_element_type=F32)
            old = top[r]
            new = jnp.maximum(old, top_of(s))
            top[r] = new
            v = kvbuf[1, row, before].reshape(BLK, HD)
            acc[r] = acc[r] * wide(jnp.exp2((old - new) * C), 2) + weigh(s, new, v)

    for off in LATE:
        sib(off).wait_recv()

    def dist(i):
        return 4 + ((i + 1) // 2) * (1 - 2 * (i % 2))

    def last_place(f):
        r = (y + dist(f // (2 * len(LATE)))) % ROWS
        zk = (z + LATE[0] + (f // 2) % len(LATE)) % COLS
        return r, base(r, zk, 3) + 2 * (f % 2), zk

    sbuf[0] = s_tile(*last_place(0))

    @pl.loop(0, ROWS)
    def _(i):
        d = dist(i)
        r = (y + d) % ROWS
        for u in range(2 * len(LATE)):
            f = 2 * len(LATE) * i + u
            sbuf[(u + 1) % 2] = s_tile(*last_place(jnp.minimum(f + 1, 2 * len(LATE) * ROWS - 1)))
            update(*last_place(f), sbuf[u % 2])
        done = acc[r]
        obuf[r] = (done[:, :HD] / done[:, HD:]).astype(BF16)

        @pl.when(d > 0)
        def _():
            ocopy(d).start()

    own_o = pltpu.make_async_copy(obuf.at[y], o_ref.at[y], loc.at[2])
    own_o.start()

    for d in order:
        kva(d).wait_send()
        qcopy(d).wait_send()
        cycopy(d).wait_send()
        czcopy(d).wait_send()
    for way in ways:
        for hop in (1, 2, 3):
            vz(way, hop).wait_send()
            for piece in range(4):
                kz(way, hop, piece).wait_send()
        vz(way, 4, way).wait_send()
        for piece in (2 * way, 2 * way + 1):
            kz(way, 4, piece).wait_send()
    for d in near:
        x0(0, d).wait_send()
        x0(1, d).wait_send()
        for off in range(1, COLS):
            vx(off, d).wait_send()
    for off in range(COLS):
        sib(off).wait_send()
    own_o.wait()
    for d in order:
        ocopy(d).wait()


def attend(queries, keys, values, doc_ids):
    qs = queries.reshape(TOK, ROWS, PG, HD).transpose(1, 0, 2, 3).reshape(ROWS, QROWS, HD)
    kvs = jnp.stack([keys, values]).transpose(2, 0, 1, 3)
    dma = pltpu.SemaphoreType.DMA
    vmem = pl.BlockSpec(memory_space=pltpu.VMEM)
    out = pl.pallas_call(
        kernel,
        out_shape=jax.ShapeDtypeStruct((ROWS, QROWS, HD), BF16),
        in_specs=[vmem, vmem, vmem],
        out_specs=pl.BlockSpec(memory_space=pl.ANY),
        scratch_shapes=[
            pltpu.VMEM((ROWS, QROWS, HD), BF16),
            pltpu.VMEM((2, ROWS, COLS, XS, CS, TOK, HD), BF16),
            pltpu.VMEM((ROWS, QROWS, HD), BF16),
            pltpu.VMEM((COLS, ROWS, BLK, HD), BF16),
            pltpu.VMEM((ROWS, QROWS, 2 * HD), F32),
            pltpu.VMEM((ROWS, QROWS, HD), F32),
            pltpu.VMEM((2, QROWS, 2 * BLK), F32),
            pltpu.VMEM((ROWS, QROWS, HD), BF16),
            pltpu.VMEM((ROWS, 8, HD), jnp.int32),
            pltpu.VMEM((COLS, 8, HD), jnp.int32),
            dma((3,)),
            *[dma((8,))] * 10,
            *[dma((2, 4))] * 2,
            *[dma((2, 5))] * 2,
            *[dma((2, 5, 4))] * 2,
            *[dma((8, 4))] * 2,
            *[dma((8,))] * 2,
        ],
        compiler_params=pltpu.CompilerParams(
            collective_id=0, has_side_effects=True, vmem_limit_bytes=50 * 2**20
        ),
        name="attend",
    )(qs, kvs, doc_ids.reshape(2, HD))
    return out.reshape(ROWS, TOK, PG, HD).transpose(1, 0, 2, 3).reshape(TOK, ROWS * PG, HD)


def solution(mesh):
    tokens = P(("ctx", "kv"), None, None)
    return jax.shard_map(
        attend,
        mesh=mesh,
        in_specs=(tokens, tokens, tokens, P("ctx")),
        out_specs=tokens,
        check_vma=False,
    )
```

```python
import math

import jax
import jax.numpy as jnp
from jax import lax
from jax.experimental import pallas as pl
from jax.experimental.pallas import tpu as pltpu
from jax.sharding import PartitionSpec as P

ROWS, COLS, XS, CS = 8, 8, 4, 2
TOK, HD, PG = 32, 128, 8
QROWS = TOK * PG
BLK = XS * CS * TOK
ROWTOK = COLS * BLK
DOCS = 16
BIG = 1e30
C = math.log2(math.e) / math.sqrt(HD)
MESH = pl.DeviceIdType.MESH
F32, BF16 = jnp.float32, jnp.bfloat16
NT = (((1,), (1,)), ((), ()))
NN = (((1,), (0,)), ((), ()))


LATE = (3, 4, 5)


def wide(x, k):
    return jnp.concatenate([x] * k, axis=1)


def kernel(
    qs, kvs, ids, o_ref,
    qbuf, kvbuf, qa, kaug, acc, top, sbuf, obuf, cy, cz,
    loc, kva_s, kva_r, q_s, q_r, cy_s, cy_r, cz_s, cz_r, o_s, o_r,
    x0_s, x0_r, vz_s, vz_r, kz_s, kz_r, vx_s, vx_r, sib_s, sib_r,
):
    ctx, kv = lax.axis_index("ctx"), lax.axis_index("kv")
    y, z, x, c = ctx // COLS, ctx % COLS, kv // CS, kv % CS

    def on_y(d):
        return (((y + d) % ROWS) * COLS + z, kv)

    def on_z(d):
        return (y * COLS + (z + d) % COLS, kv)

    def on_x(d):
        return (ctx, ((x + d) % XS) * CS + c)

    sibling = (ctx, x * CS + 1 - c)

    def remote(src, dst, ss, rs, dev):
        return pltpu.make_async_remote_copy(
            src_ref=src, dst_ref=dst, send_sem=ss, recv_sem=rs, device_id=dev, device_id_type=MESH
        )

    def kva(d):
        return remote(kvs.at[(y + d) % ROWS], kvbuf.at[:, y, z, x, c], kva_s.at[d], kva_r.at[d], on_y(d))

    def qcopy(d):
        return remote(qs.at[(y + d) % ROWS], qbuf.at[y], q_s.at[d], q_r.at[d], on_y(d))

    def cycopy(d):
        return remote(cy.at[y], cy.at[y], cy_s.at[d], cy_r.at[d], on_y(d))

    def czcopy(d):
        return remote(cz.at[z], cz.at[z], cz_s.at[d], cz_r.at[d], on_z(d))

    def x0(which, d):
        at = kvbuf.at[which, :, z, x, c]
        return remote(at, at, x0_s.at[which, d], x0_r.at[which, d], on_x(d))

    def rows_of(half):
        return pl.ds(0, ROWS) if half is None else pl.ds(half * (ROWS // 2), ROWS // 2)

    def column(way, hop):
        return (z + (COLS + 1 - hop if way == 0 else hop - 1)) % COLS

    def vz(way, hop, half=None):
        at = kvbuf.at[1, rows_of(half), column(way, hop), x, c]
        return remote(at, at, vz_s.at[way, hop], vz_r.at[way, hop], on_z(1 if way == 0 else COLS - 1))

    def kz(way, hop, piece):
        at = kvbuf.at[0, :, column(way, hop), (x + (0, 3, 1, 2)[piece]) % XS, c]
        return remote(
            at, at, kz_s.at[way, hop, piece], kz_r.at[way, hop, piece], on_z(1 if way == 0 else COLS - 1)
        )

    def vx(off, d):
        at = kvbuf.at[1, :, (z + off) % COLS, x, c]
        return remote(at, at, vx_s.at[off, d], vx_r.at[off, d], on_x(d))

    def sib(off):
        at = kvbuf.at[:, :, (z + off) % COLS, :, c]
        return remote(at, at, sib_s.at[off], sib_r.at[off], sibling)

    def ocopy(d):
        return remote(obuf.at[(y + d) % ROWS], o_ref.at[y], o_s.at[d], o_r.at[d], on_y(d))

    barrier = pltpu.get_barrier_semaphore()
    peers = [on_y(d) for d in range(1, ROWS)] + [on_z(d) for d in range(1, COLS)]
    peers += [on_x(d) for d in range(1, XS)] + [sibling]
    for dev in peers:
        pl.semaphore_signal(barrier, inc=1, device_id=dev, device_id_type=MESH)

    lane = lax.broadcasted_iota(jnp.int32, (1, HD), 1)
    below = jnp.where(lane == 0, 0, BLK)
    upto = jnp.full((1, HD), BLK, jnp.int32)
    for d in range(1, DOCS):
        count = jnp.sum(jnp.where(ids[...] < d, 1.0, 0.0), axis=1, keepdims=True)
        count = jnp.sum(count, axis=0, keepdims=True).astype(jnp.int32)
        below = jnp.where(lane == d, count, below)
        upto = jnp.where(lane == d - 1, count, upto)
    row8 = lax.broadcasted_iota(jnp.int32, (8, HD), 0)
    cy[y] = jnp.where(row8 < 4, below, upto)

    pl.semaphore_wait(barrier, len(peers))

    order = (1, 7, 2, 6, 3, 5, 4)
    near = (1, 3, 2)
    ways = (0, 1)
    for d in order:
        kva(d).start()
    for d in order:
        cycopy(d).start()
    own_kv = pltpu.make_async_copy(kvs.at[y], kvbuf.at[:, y, z, x, c], loc.at[0])
    own_q = pltpu.make_async_copy(qs.at[y], qbuf.at[y], loc.at[1])
    own_kv.start()
    own_q.start()
    for d in order:
        qcopy(d).start()
    for d in order:
        kva(d).wait_recv()
    own_kv.wait()

    for way in ways:
        vz(way, 1).start()
    for d in near:
        x0(0, d).start()
    for way in ways:
        kz(way, 1, 0).start()
    for d in near:
        x0(1, d).start()
    for d in order:
        cycopy(d).wait_recv()
    line = cy[0]
    for r in range(1, ROWS):
        line = line + cy[r]
    cz[z] = line
    for d in order:
        czcopy(d).start()
    for piece in (1, 2, 3):
        x0(0, near[piece - 1]).wait_recv()
        for way in ways:
            kz(way, 1, piece).start()

    def v_event(hop):
        for way in ways:
            if hop < 4:
                vz(way, hop).wait_recv()
            else:
                vz(way, 4, way).wait_recv()
            if hop < 3:
                vz(way, hop + 1).start()
            elif hop == 3:
                vz(way, 4, way).start()
        for off in (COLS - hop, hop) if hop < 4 else (4,):
            for d in near:
                vx(off, d).start()

    def k_event(hop, pieces):
        mine = 0 if pieces[0] == 0 else 1
        for piece in pieces:
            for way in ways:
                if hop < 4 or way == mine:
                    kz(way, hop, piece).wait_recv()
                if hop < 3 or (hop == 3 and way == mine):
                    kz(way, hop + 1, piece).start()

    def pass_on(off):
        for d in near:
            vx(off, d).wait_recv()
        sib(off).start()

    v_event(1)
    for d in order:
        czcopy(d).wait_recv()
    total = cz[0]
    for r in range(1, COLS):
        total = total + cz[r]
    first, last = total[0:1], total[4:5]
    sign = jnp.where(lane < DOCS, 1, -1)
    row256 = lax.broadcasted_iota(jnp.int32, (BLK, HD), 0)
    here = BLK * z + (CS * TOK) * x + TOK * c

    @pl.loop(0, ROWS)
    def _(r):
        pos = ROWTOK * r + here + row256 // PG
        same = (pos >= first) & (pos < last) & (lane < DOCS)
        qa[r] = jnp.where(same | (lane == DOCS + r), -BIG, 0.0).astype(BF16)

    @pl.loop(0, COLS)
    def _(zk):
        bound = ROWTOK * (lane - DOCS + jnp.where(zk < z, 1, 0))
        limit = jnp.where(lane < DOCS, first, 1 - bound)

        @pl.loop(0, ROWS)
        def _(r):
            pos = ROWTOK * r + BLK * zk + row256
            kaug[zk, r] = jnp.where(pos * sign < limit, 1.0, 0.0).astype(BF16)

    k_event(1, (0, 1))
    for d in near:
        x0(1, d).wait_recv()
    sib(0).start()

    v_event(2)
    sib(0).wait_recv()

    def s_tile(r, r0, zk):
        q = jnp.concatenate([qbuf[r], qa[r]], axis=1)
        k = kvbuf[0, pl.ds(r0, 2), zk].reshape(2 * BLK, HD)
        k = jnp.concatenate([k, kaug[zk, pl.ds(r0, 2)].reshape(2 * BLK, HD)], axis=1)
        return lax.dot_general(q, k, NT, preferred_element_type=F32)

    def v_tile(r0, zk):
        return kvbuf[1, pl.ds(r0, 2), zk].reshape(2 * BLK, HD)

    def top_of(s):
        mx = s[:, :HD]
        for j in range(1, s.shape[1] // HD):
            mx = jnp.maximum(mx, s[:, j * HD:(j + 1) * HD])
        return jnp.max(mx, axis=1, keepdims=True)

    def weigh(s, mn, v):
        p = jnp.exp2((s - wide(mn, s.shape[1] // HD)) * C).astype(BF16)
        v = jnp.concatenate([v, jnp.ones_like(v)], axis=1)
        return lax.dot_general(p, v, NN, preferred_element_type=F32)

    def update(r, r0, zk, s):
        old = top[r]
        new = jnp.maximum(old, top_of(s))
        fade = jnp.exp2((old - new) * C)
        top[r] = new
        acc[r] = acc[r] * wide(fade, 2) + weigh(s, new, v_tile(r0, zk))

    def base(r, zk, spread):
        high = r - jnp.where(zk < z, 0, 1)
        return jnp.maximum(high - spread, 0)

    def arrive(i):
        half = (i + 1) // 2
        d = (half + (i + 1) % 2 * (COLS - 2 * half)) % ROWS

        @pl.when(i == 0)
        def _():
            own_q.wait()

        @pl.when(i > 0)
        def _():
            qcopy(d).wait_recv()

        return (y + ROWS - d) % ROWS

    @pl.loop(0, ROWS // 2)
    def _(pair):
        parts = [arrive(2 * pair), arrive(2 * pair + 1)]
        at = (CS * TOK) * x + TOK * c + lax.broadcasted_iota(jnp.int32, (QROWS, BLK), 0) // PG
        causal = lax.broadcasted_iota(jnp.int32, (QROWS, BLK), 1) <= at
        scores = []
        for r in parts:
            q = jnp.concatenate([qbuf[r], jnp.where(lane < DOCS, qa[r], 0.0).astype(BF16)], axis=1)
            k = jnp.concatenate([kvbuf[0, r, z].reshape(BLK, HD), kaug[z, r]], axis=1)
            s = lax.dot_general(q, k, NT, preferred_element_type=F32)
            r0 = base(r, z, 3)
            scores.append((r, r0, jnp.where(causal, s, -BIG), s_tile(r, r0, z), s_tile(r, r0 + 2, z)))
        for r, r0, s, s1, s2 in scores:
            new = jnp.maximum(jnp.maximum(top_of(s), top_of(s1)), top_of(s2))
            new = jnp.broadcast_to(new, (QROWS, HD))
            top[r] = new
            acc[r] = (
                weigh(s, new, kvbuf[1, r, z].reshape(BLK, HD))
                + weigh(s1, new, v_tile(r0, z))
                + weigh(s2, new, v_tile(r0 + 2, z))
            )

        @pl.when(pair == 0)
        def _():
            k_event(1, (2, 3))

        @pl.when(pair == 1)
        def _():
            v_event(3)

        @pl.when(pair == 2)
        def _():
            pass_on(7)

    pass_on(1)
    k_event(2, (0, 1))

    def run(place, tiles):
        sbuf[0] = s_tile(*place(0))
        for f in range(tiles):
            if f + 1 < tiles:
                sbuf[(f + 1) % 2] = s_tile(*place(f + 1))
            update(*place(f), sbuf[f % 2])

    @pl.loop(0, 4)
    def _(g):
        off = jnp.where(g % 2 == 0, COLS - 1 - g // 2, 1 + g // 2)
        zk = (z + off) % COLS
        sib(off).wait_recv()

        def place(f):
            r = f if f < 2 else 2 + (f - 2) // 2
            return r, base(r, zk, 3) + (0 if f < 2 else 2 * (f % 2)), zk

        run(place, 14)

        @pl.when(g == 0)
        def _():
            k_event(2, (2, 3))
            v_event(4)
            pass_on(6)

        @pl.when(g == 1)
        def _():
            k_event(3, (0, 1))
            pass_on(2)

        @pl.when(g == 2)
        def _():
            k_event(3, (2, 3))
            pass_on(5)

        @pl.when(g == 3)
        def _():
            k_event(4, (0, 1))
            k_event(4, (2, 3))
            pass_on(3)
            pass_on(4)

    before = (z + COLS - 1) % COLS

    @pl.loop(4, ROWS)
    def _(r):
        row = r - 4 - jnp.where(before < z, 0, 1)

        @pl.when(row >= 0)
        def _():
            q = jnp.concatenate([qbuf[r], qa[r]], axis=1)
            k = jnp.concatenate([kvbuf[0, row, before].reshape(BLK, HD), kaug[before, row]], axis=1)
            s = lax.dot_general(q, k, NT, preferred_element_type=F32)
            old = top[r]
            new = jnp.maximum(old, top_of(s))
            top[r] = new
            v = kvbuf[1, row, before].reshape(BLK, HD)
            acc[r] = acc[r] * wide(jnp.exp2((old - new) * C), 2) + weigh(s, new, v)

    for off in LATE:
        sib(off).wait_recv()

    def dist(i):
        return 4 + ((i + 1) // 2) * (1 - 2 * (i % 2))

    def last_place(f):
        r = (y + dist(f // (2 * len(LATE)))) % ROWS
        zk = (z + LATE[0] + (f // 2) % len(LATE)) % COLS
        return r, base(r, zk, 3) + 2 * (f % 2), zk

    sbuf[0] = s_tile(*last_place(0))

    @pl.loop(0, ROWS // 2)
    def _(pair):
        for i, shift in ((2 * pair, 0), (2 * pair + 1, 2 * len(LATE))):
            d = dist(i)
            r = (y + d) % ROWS
            for u in range(2 * len(LATE)):
                f = 4 * len(LATE) * pair + shift + u
                sbuf[(u + 1) % 2] = s_tile(*last_place(jnp.minimum(f + 1, 2 * len(LATE) * ROWS - 1)))
                update(*last_place(f), sbuf[u % 2])
            done = acc[r]
            obuf[r] = (done[:, :HD] / done[:, HD:]).astype(BF16)
            if shift == 0:
                ocopy(d).start()
            else:

                @pl.when(d > 0)
                def _():
                    ocopy(d).start()

    own_o = pltpu.make_async_copy(obuf.at[y], o_ref.at[y], loc.at[2])
    own_o.start()

    for d in order:
        kva(d).wait_send()
        qcopy(d).wait_send()
        cycopy(d).wait_send()
        czcopy(d).wait_send()
    for way in ways:
        for hop in (1, 2, 3):
            vz(way, hop).wait_send()
            for piece in range(4):
                kz(way, hop, piece).wait_send()
        vz(way, 4, way).wait_send()
        for piece in (2 * way, 2 * way + 1):
            kz(way, 4, piece).wait_send()
    for d in near:
        x0(0, d).wait_send()
        x0(1, d).wait_send()
        for off in range(1, COLS):
            vx(off, d).wait_send()
    for off in range(COLS):
        sib(off).wait_send()
    own_o.wait()
    for d in order:
        ocopy(d).wait()


def attend(queries, keys, values, doc_ids):
    qs = queries.reshape(TOK, ROWS, PG, HD).transpose(1, 0, 2, 3).reshape(ROWS, QROWS, HD)
    kvs = jnp.stack([keys, values]).transpose(2, 0, 1, 3)
    dma = pltpu.SemaphoreType.DMA
    vmem = pl.BlockSpec(memory_space=pltpu.VMEM)
    out = pl.pallas_call(
        kernel,
        out_shape=jax.ShapeDtypeStruct((ROWS, QROWS, HD), BF16),
        in_specs=[vmem, vmem, vmem],
        out_specs=pl.BlockSpec(memory_space=pl.ANY),
        scratch_shapes=[
            pltpu.VMEM((ROWS, QROWS, HD), BF16),
            pltpu.VMEM((2, ROWS, COLS, XS, CS, TOK, HD), BF16),
            pltpu.VMEM((ROWS, QROWS, HD), BF16),
            pltpu.VMEM((COLS, ROWS, BLK, HD), BF16),
            pltpu.VMEM((ROWS, QROWS, 2 * HD), F32),
            pltpu.VMEM((ROWS, QROWS, HD), F32),
            pltpu.VMEM((2, QROWS, 2 * BLK), F32),
            pltpu.VMEM((ROWS, QROWS, HD), BF16),
            pltpu.VMEM((ROWS, 8, HD), jnp.int32),
            pltpu.VMEM((COLS, 8, HD), jnp.int32),
            dma((3,)),
            *[dma((8,))] * 10,
            *[dma((2, 4))] * 2,
            *[dma((2, 5))] * 2,
            *[dma((2, 5, 4))] * 2,
            *[dma((8, 4))] * 2,
            *[dma((8,))] * 2,
        ],
        compiler_params=pltpu.CompilerParams(
            collective_id=0, has_side_effects=True, vmem_limit_bytes=50 * 2**20
        ),
        name="attend",
    )(qs, kvs, doc_ids.reshape(2, HD))
    return out.reshape(ROWS, TOK, PG, HD).transpose(1, 0, 2, 3).reshape(TOK, ROWS * PG, HD)


def solution(mesh):
    tokens = P(("ctx", "kv"), None, None)
    return jax.shard_map(
        attend,
        mesh=mesh,
        in_specs=(tokens, tokens, tokens, P("ctx")),
        out_specs=tokens,
        check_vma=False,
    )
```
